512 devices in a mesh: gx: 16 (over y_hi, x, core), gy: 8 (over z), gz: 4 (over y_lo).
Axes of the slice: x: 4, y: 8 (y_hi: 2, y_lo: 4; y = y_hi * 4 + y_lo), z: 8, core: 2. Of those that a mesh axis runs over, the one named last changes fastest.
Arguments:
- block_input: bfloat16 [1024, 14848], P('gx', ('gy', 'gz')), may hold values from -6 to 6
- context: bfloat16 [1024, 7424], P('gx', ('gy', 'gz')), may hold values from -6 to 6
- query_grad: bfloat16 [1024, 7424], P(('gy', 'gz'), 'gx'), may hold values from -6 to 6
- output_grad: bfloat16 [1024, 14848], P(('gy', 'gz'), 'gx'), may hold values from -6 to 6
- query_weight: bfloat16 [14848, 7424], P(('gy', 'gz'), 'gx'), may hold values from -0.046875 to 0.046875
- query_moment: bfloat16 [14848, 7424], P(('gy', 'gz'), 'gx'), may hold values from -0.59765625 to 0.59765625
- output_weight: bfloat16 [7424, 14848], P(('gy', 'gz'), 'gx'), may hold values from -0.0625 to 0.0625
- output_moment: bfloat16 [7424, 14848], P(('gy', 'gz'), 'gx'), may hold values from -0.59765625 to 0.59765625
Outputs:
- input_grad: bfloat16 [1024, 14848], P('gx', ('gy', 'gz'))
- context_grad: bfloat16 [1024, 7424], P('gx', ('gy', 'gz'))
- query_step: bfloat16 [14848, 7424], P(('gy', 'gz'), 'gx')
- query_momentum: bfloat16 [14848, 7424], P(('gy', 'gz'), 'gx')
- output_step: bfloat16 [7424, 14848], P(('gy', 'gz'), 'gx')
- output_momentum: bfloat16 [7424, 14848], P(('gy', 'gz'), 'gx')
The draws below stay inside these ranges and needn't reach their ends.
All inputs are finite; a program needn't handle non-finite values.
Results may differ from the reference program's by a relative error of at most 0.001.
Values may be sent and summed in bfloat16 or wider, within the bound.
No kernel may reach another device: no remote copies, remote signals or barrier semaphores. Data moves between devices by JAX's collectives and lax.ppermute only.
A program may use at most 64 MiB of HBM per device.

```python
import math
import jax
import jax.numpy as jnp

D = 14848
TOKENS = 1024
HD = 7424


def steps_of(key, dims, pieces, low, high):
    def one(dim, shards_of):
        steps = jax.random.uniform(jax.random.fold_in(jax.random.fold_in(key, 6), dim), (shards_of,), jnp.float32, low / len(pieces), high / len(pieces))
        return jnp.repeat(jnp.exp(steps), dims[dim] // shards_of).reshape((-1,) + (1,) * (len(dims) - dim - 1))

    gain = one(*pieces[0])
    for cut in pieces[1:]:
        gain = gain * one(*cut)
    return gain


def bell_draw(own_key, dims, width, bound, split=(), held_as=jnp.bfloat16):
    loudness = steps_of(own_key, dims, split, -0.22, 0.18) if split else 1.0
    drawn = jax.random.normal(own_key, dims, jnp.float32) * width * loudness
    return jnp.minimum(jnp.maximum(drawn, -bound), bound).astype(held_as)


def setup_inputs(seed: int = 0) -> dict:
    streams_of = jax.random.split(jax.random.key(seed), 9)
    block_input = bell_draw(streams_of[0], (TOKENS, D), 1.0, 6.0, ((0, 16), (1, 32)))
    context = bell_draw(streams_of[1], (TOKENS, HD), 1.0, 6.0, ((0, 16), (1, 32)))
    query_grad = bell_draw(streams_of[2], (TOKENS, HD), 1.0, 6.0, ((0, 32), (1, 16)))
    output_grad = bell_draw(streams_of[3], (TOKENS, D), 1.0, 6.0, ((0, 32), (1, 16)))
    query_weight = bell_draw(streams_of[4], (D, HD), D ** -0.5, 0.046875, ((0, 32), (1, 16)))
    query_moment = bell_draw(streams_of[5], (D, HD), 0.1, 0.59765625, ((0, 32), (1, 16)))
    output_weight = bell_draw(streams_of[6], (HD, D), HD ** -0.5, 0.0625, ((0, 32), (1, 16)))
    output_moment = bell_draw(streams_of[7], (HD, D), 0.1, 0.59765625, ((0, 32), (1, 16)))
    return {"block_input": block_input, "context": context, "query_grad": query_grad, "output_grad": output_grad, "query_weight": query_weight, "query_moment": query_moment, "output_weight": output_weight, "output_moment": output_moment}


def lion_step(gradient, moment):
    held = moment.astype(jnp.float32)
    blended = 0.9 * held + 0.1 * gradient
    direction = blended / jnp.sqrt(blended * blended + 0.01)
    updated = 0.99 * held + 0.01 * gradient
    return (direction.astype(jnp.bfloat16), updated.astype(jnp.bfloat16))

def reference(block_input, context, query_grad, output_grad, query_weight, query_moment, output_weight, output_moment):
    norm_factor = 1.0 / math.sqrt(TOKENS)
    query_wgrad = jnp.dot(block_input.T, query_grad, preferred_element_type=jnp.float32) * norm_factor
    output_wgrad = jnp.dot(context.T, output_grad, preferred_element_type=jnp.float32) * norm_factor
    input_grad = jnp.dot(query_grad, query_weight.T, preferred_element_type=jnp.float32).astype(jnp.bfloat16)
    context_grad = jnp.dot(output_grad, output_weight.T, preferred_element_type=jnp.float32).astype(jnp.bfloat16)
    query_step, query_momentum = lion_step(query_wgrad, query_moment)
    output_step, output_momentum = lion_step(output_wgrad, output_moment)
    return (input_grad, context_grad, query_step, query_momentum, output_step, output_momentum)
```

```python
import math

import jax
import jax.numpy as jnp
from jax import lax
from jax.sharding import Mesh, PartitionSpec as P

GX, GYZ = ("yh", "x", "core"), ("z", "yl")
SWAP = [(0, 1), (1, 0)]
PAD = 512


def lion_step(gradient, moment):
    held = moment.astype(jnp.float32)
    blended = 0.9 * held + 0.1 * gradient
    direction = blended / jnp.sqrt(blended * blended + 0.01)
    updated = 0.99 * held + 0.01 * gradient
    return (direction.astype(jnp.bfloat16), updated.astype(jnp.bfloat16))


def times_transposed(left, right):
    return lax.dot_general(
        left, right, (((1,), (1,)), ((), ())), preferred_element_type=jnp.float32
    )


def rows_product(left, right):
    return lax.dot_general(
        left, right, (((0,), (0,)), ((), ())), preferred_element_type=jnp.float32
    )


def side_by_side(left, right):
    gap = jnp.zeros((left.shape[0], PAD - left.shape[1]), left.dtype)
    return jnp.concatenate([left, gap, right], axis=1)


def in_order(index, mine, theirs, axis):
    first = jnp.where(index == 0, mine, theirs)
    second = jnp.where(index == 0, theirs, mine)
    return jnp.stack([first, second], axis=axis)


def reduce_scatter(grads, weight, core):
    tokens, width = grads.shape
    chips = tokens // 128
    by_core = grads.reshape(chips, 2, 64, width)
    theirs = lax.dynamic_index_in_dim(by_core, 1 - core, 1, keepdims=False)
    mine = lax.dynamic_index_in_dim(by_core, core, 1, keepdims=False)
    sent = times_transposed(theirs.reshape(-1, width), weight)
    kept = times_transposed(mine.reshape(-1, width), weight)
    pair = kept + lax.ppermute(sent, "core", SWAP)
    parts = lax.all_to_all(
        pair.reshape(chips, 64, -1), ("yh", "x"), 0, 0, tiled=True
    )
    return jnp.sum(parts, axis=0).astype(jnp.bfloat16)


def on_device(
    block_input,
    context,
    query_grad,
    output_grad,
    query_weight,
    query_moment,
    output_weight,
    output_moment,
):
    core, yh = lax.axis_index("core"), lax.axis_index("yh")
    inputs = side_by_side(block_input, context)
    inputs = in_order(yh, inputs, lax.ppermute(inputs, "yh", SWAP), 0)
    grads = lax.all_gather(
        side_by_side(query_grad, output_grad), "yl", axis=0, tiled=True
    )
    output_all = lax.all_gather(grads[:, PAD:], "z", axis=0, tiled=True)
    query_all = lax.all_gather(
        grads[:, : query_grad.shape[1]], "z", axis=0, tiled=True
    )
    inputs = lax.all_to_all(
        jnp.broadcast_to(inputs[None], (4,) + inputs.shape), "x", 0, 0, tiled=True
    )
    inputs = jnp.swapaxes(inputs, 0, 1)
    inputs = in_order(core, inputs, lax.ppermute(inputs, "core", SWAP), 2)
    inputs = inputs.reshape(-1, inputs.shape[-1])
    input_all, context_all = inputs[:, : block_input.shape[1]], inputs[:, PAD:]

    input_grad = reduce_scatter(query_all, query_weight, core)
    context_grad = reduce_scatter(output_all, output_weight, core)
    norm_factor = 1.0 / math.sqrt(float(query_all.shape[0]))
    query_step, query_momentum = lion_step(
        rows_product(input_all, query_all) * norm_factor, query_moment
    )
    output_step, output_momentum = lion_step(
        rows_product(context_all, output_all) * norm_factor, output_moment
    )
    return (
        input_grad,
        context_grad,
        query_step,
        query_momentum,
        output_step,
        output_momentum,
    )


def solution(mesh):
    split = Mesh(mesh.devices.reshape(2, 4, 2, 8, 4), GX + GYZ)
    rows, columns = P(GX, GYZ), P(GYZ, GX)
    return jax.shard_map(
        on_device,
        mesh=split,
        in_specs=(rows, rows) + (columns,) * 6,
        out_specs=(rows, rows) + (columns,) * 4,
        check_vma=False,
    )
```

```python
import functools
import math

import jax
import jax.numpy as jnp
from jax import lax
from jax.experimental import pallas as pl
from jax.experimental.pallas import tpu as pltpu
from jax.sharding import Mesh, PartitionSpec as P

GX, GYZ = ("yh", "x", "core"), ("z", "yl")
SWAP = [(0, 1), (1, 0)]
PAD = 512
MIB = 2**20


def times_transposed(left, right):
    return lax.dot_general(
        left, right, (((1,), (1,)), ((), ())), preferred_element_type=jnp.float32
    )


def rows_product(left, right):
    return lax.dot_general(
        left, right, (((0,), (0,)), ((), ())), preferred_element_type=jnp.float32
    )


def lanes(columns):
    return -(-columns // 128) * 128


def side_by_side(left, right):
    gap = jnp.zeros((left.shape[0], PAD - left.shape[1]), left.dtype)
    return jnp.concatenate([left, gap, right], axis=1)


def call(kernel, out_shapes, out_specs, in_specs, pick, *operands, flops=0):
    whole = lambda array: pl.BlockSpec(array.shape, lambda i, pick: (0,) * array.ndim)
    moved = sum(o.size * o.dtype.itemsize for o in operands)
    return pl.pallas_call(
        kernel,
        grid_spec=pltpu.PrefetchScalarGridSpec(
            num_scalar_prefetch=1,
            grid=(1,),
            in_specs=[spec or whole(o) for spec, o in zip(in_specs, operands)],
            out_specs=[spec or whole(o) for spec, o in zip(out_specs, out_shapes)],
        ),
        out_shape=out_shapes,
        compiler_params=pltpu.CompilerParams(vmem_limit_bytes=20 * MIB),
        cost_estimate=pl.CostEstimate(
            flops=flops, bytes_accessed=moved, transcendentals=0
        ),
    )(pick, *operands)


def product_kernel(x_first, pick, grads, weight, *rest):
    out, received = rest[-1], rest[:-1]
    product = times_transposed(grads[...].reshape(-1, grads.shape[-1]), weight[...])
    features = product.shape[1]
    if received:
        product = product + received[0][:, :features]
    if x_first:
        blocks = product.reshape(2, 4, 64, features)
        for yh in range(2):
            for x in range(4):
                out[x, yh, :, :features] = blocks[yh, x]
        out[:, :, :, features:] = jnp.zeros(
            (4, 2, 64, out.shape[-1] - features), jnp.float32
        )
    else:
        out[:, :features] = product
        out[:, features:] = jnp.zeros(
            (out.shape[0], out.shape[1] - features), jnp.float32
        )


def token_half(half, grads, weight, *received, x_first=False):
    tokens, width = grads.shape
    chips, columns = tokens // 128, lanes(weight.shape[0])
    shape = (4, 2, 64, columns) if x_first else (chips * 64, columns)
    return call(
        functools.partial(product_kernel, x_first),
        [jax.ShapeDtypeStruct(shape, jnp.float32)],
        [None],
        [pl.BlockSpec((chips, 1, 64, width), lambda i, pick: (0, pick[0], 0, 0)), None]
        + [None] * len(received),
        half.reshape(1),
        grads.reshape(chips, 2, 64, width),
        weight,
        *received,
        flops=2 * chips * 64 * columns * width,
    )[0]


def sum_along_x_kernel(pick, near_parts, far_parts, near, far):
    near[...] = jnp.sum(near_parts[...], axis=(0, 1))
    far[...] = jnp.sum(far_parts[...], axis=(0, 1))


def sum_along_x(yh, parts):
    block = (4, 1, 64, parts.shape[-1])
    shape = jax.ShapeDtypeStruct((64, parts.shape[-1]), jnp.float32)
    return call(
        sum_along_x_kernel,
        [shape] * 2,
        [None] * 2,
        [
            pl.BlockSpec(block, lambda i, pick: (0, pick[0], 0, 0)),
            pl.BlockSpec(block, lambda i, pick: (0, 1 - pick[0], 0, 0)),
        ],
        yh.reshape(1),
        parts,
        parts,
    )


def total_kernel(pick, parts, out):
    features = out.shape[-1]
    out[...] = jnp.sum(parts[...], axis=0)[:, :features].astype(jnp.bfloat16)


def total(parts, features):
    return call(
        total_kernel,
        [jax.ShapeDtypeStruct((parts.shape[1], features), jnp.bfloat16)],
        [None],
        [None],
        jnp.zeros((1,), jnp.int32),
        parts,
    )[0]


def momentum_kernel(
    first, pick, inputs, inputs_theirs, grads, grads_theirs, moment, step, momentum
):
    rows = pl.ds(first, moment.shape[0])
    tokens = grads.shape[0] * grads.shape[2]
    width = grads.shape[-1]
    gradient = rows_product(
        inputs[..., rows].reshape(tokens, -1), grads[...].reshape(tokens, width)
    ) + rows_product(
        inputs_theirs[..., rows].reshape(tokens, -1),
        grads_theirs[...].reshape(tokens, width),
    )
    gradient = gradient * (1.0 / math.sqrt(float(2 * tokens)))
    held = moment[...].astype(jnp.float32)
    blended = 0.9 * held + 0.1 * gradient
    step[...] = (blended / jnp.sqrt(blended * blended + 0.01)).astype(jnp.bfloat16)
    momentum[...] = (0.99 * held + 0.01 * gradient).astype(jnp.bfloat16)


def momentum_step(core, inputs, inputs_theirs, first, grads, moment):
    tokens, width = grads.shape
    grads = grads.reshape(tokens // 128, 2, 64, width)
    block = (tokens // 128, 1, 64, width)
    return call(
        functools.partial(momentum_kernel, first),
        [jax.ShapeDtypeStruct(moment.shape, jnp.bfloat16)] * 2,
        [None] * 2,
        [
            None,
            None,
            pl.BlockSpec(block, lambda i, pick: (0, pick[0], 0, 0)),
            pl.BlockSpec(block, lambda i, pick: (0, 1 - pick[0], 0, 0)),
            None,
        ],
        core.reshape(1),
        inputs,
        inputs_theirs,
        grads,
        grads,
        moment,
        flops=2 * tokens * moment.size,
    )


def on_device(
    block_input,
    context,
    query_grad,
    output_grad,
    query_weight,
    query_moment,
    output_weight,
    output_moment,
):
    core, yh = lax.axis_index("core"), lax.axis_index("yh")
    width = query_grad.shape[1]
    grads = side_by_side(query_grad, output_grad)
    grads = lax.all_gather(grads, "yl", axis=0, tiled=True)
    inputs = side_by_side(block_input, context)
    grads, inputs = lax.optimization_barrier((grads, inputs))
    output_all = lax.all_gather(grads[:, PAD:], "z", axis=0, tiled=True)
    inputs = jnp.broadcast_to(inputs[None], (8,) + inputs.shape)
    inputs = lax.all_to_all(inputs, ("yh", "x"), 0, 0, tiled=True)
    query_all = lax.all_gather(grads[:, :width], "z", axis=0, tiled=True)
    query_all, inputs = lax.optimization_barrier((query_all, inputs))
    query_theirs = token_half(1 - core, query_all, query_weight)
    query_theirs = lax.ppermute(query_theirs, "core", SWAP)
    inputs_theirs = lax.ppermute(inputs, "core", SWAP)
    query_pair = token_half(core, query_all, query_weight, query_theirs, x_first=True)
    query_parts = lax.all_to_all(query_pair, "x", 0, 0, tiled=True)
    output_theirs = token_half(1 - core, output_all, output_weight)
    output_theirs = lax.ppermute(output_theirs, "core", SWAP)
    output_pair = token_half(core, output_all, output_weight, output_theirs)
    query_parts, output_pair = lax.optimization_barrier((query_parts, output_pair))
    output_pair = output_pair.reshape(8, 64, output_pair.shape[-1])
    output_parts = lax.all_to_all(output_pair, ("yh", "x"), 0, 0, tiled=True)
    context_grad = total(output_parts, context.shape[1])
    query_near, query_far = sum_along_x(yh, query_parts)
    query_far = lax.ppermute(query_far, "yh", SWAP)
    input_grad = (query_near + query_far)[:, : block_input.shape[1]]
    input_grad = input_grad.astype(jnp.bfloat16)
    query_step, query_momentum = momentum_step(
        core, inputs, inputs_theirs, 0, query_all, query_moment
    )
    output_step, output_momentum = momentum_step(
        core, inputs, inputs_theirs, PAD, output_all, output_moment
    )
    return (
        input_grad,
        context_grad,
        query_step,
        query_momentum,
        output_step,
        output_momentum,
    )


def solution(mesh):
    split = Mesh(mesh.devices.reshape(2, 4, 2, 8, 4), GX + GYZ)
    rows, columns = P(GX, GYZ), P(GYZ, GX)
    return jax.shard_map(
        on_device,
        mesh=split,
        in_specs=(rows, rows) + (columns,) * 6,
        out_specs=(rows, rows) + (columns,) * 4,
        check_vma=False,
    )
```

```python
import functools
import math

import jax
import jax.numpy as jnp
from jax import lax
from jax.experimental import pallas as pl
from jax.experimental.pallas import tpu as pltpu
from jax.sharding import Mesh, PartitionSpec as P

GX, GYZ = ("yh", "x", "core"), ("z", "yl")
SWAP = [(0, 1), (1, 0)]
PAD = 512
MIB = 2**20


def times_transposed(left, right):
    return lax.dot_general(
        left, right, (((1,), (1,)), ((), ())), preferred_element_type=jnp.float32
    )


def rows_product(left, right):
    return lax.dot_general(
        left, right, (((0,), (0,)), ((), ())), preferred_element_type=jnp.float32
    )


def lanes(columns):
    return -(-columns // 128) * 128


def side_by_side(left, right):
    gap = jnp.zeros((left.shape[0], PAD - left.shape[1]), left.dtype)
    return jnp.concatenate([left, gap, right], axis=1)


def call(
    kernel, out_shapes, out_specs, in_specs, pick, *operands, flops=0, scratch=()
):
    whole = lambda array: pl.BlockSpec(array.shape, lambda i, pick: (0,) * array.ndim)
    moved = sum(o.size * o.dtype.itemsize for o in operands)
    return pl.pallas_call(
        kernel,
        grid_spec=pltpu.PrefetchScalarGridSpec(
            num_scalar_prefetch=1,
            grid=(1,),
            scratch_shapes=scratch,
            in_specs=[spec or whole(o) for spec, o in zip(in_specs, operands)],
            out_specs=[spec or whole(o) for spec, o in zip(out_specs, out_shapes)],
        ),
        out_shape=out_shapes,
        compiler_params=pltpu.CompilerParams(vmem_limit_bytes=20 * MIB),
        cost_estimate=pl.CostEstimate(
            flops=flops, bytes_accessed=moved, transcendentals=0
        ),
    )(pick, *operands)


HBM = pl.BlockSpec(memory_space=pltpu.HBM)


def in_hbm(array):
    return pltpu.with_memory_space_constraint(array, pltpu.HBM)


def copy_all(pairs, semaphores):
    copies = [
        pltpu.make_async_copy(source, target, semaphores.at[i])
        for i, (source, target) in enumerate(pairs)
    ]
    for copy in copies:
        copy.start()
    for copy in copies:
        copy.wait()


def product_kernel(fetch, place, pick, grads, weight, *rest):
    rest, scratch = rest[: 1 + (place is not None)], rest[1 + (place is not None) :]
    scratch = list(scratch)
    if fetch:
        held, semaphores = scratch.pop(0), scratch.pop(0)
        copy_all([(grads.at[i, pick[0]], held.at[i]) for i in range(8)], semaphores)
    else:
        held = grads
    product = times_transposed(held[...].reshape(512, held.shape[-1]), weight[...])
    features = product.shape[1]
    out = rest[-1]
    gap = jnp.zeros((512, out.shape[-1] - features), jnp.float32)
    if place is None:
        out[:, :features] = product
        out[:, features:] = gap
        return
    sums, semaphores = scratch
    sums[:, :, :features] = (product + rest[0][:, :features]).reshape(8, 64, features)
    sums[:, :, features:] = gap.reshape(8, 64, -1)
    copy_all([(sums.at[i], out.at[place(i)]) for i in range(8)], semaphores)


def x_yh(chip):
    return (chip % 4, chip // 4)


def in_turn(chip):
    return (chip,)


def token_half(half, grads, weight, *received, fetch=False, place=None):
    tokens, width = grads.shape
    columns = lanes(weight.shape[0])
    grads = grads.reshape(8, 2, 64, width)
    eight = pltpu.SemaphoreType.DMA((8,))
    scratch = [pltpu.VMEM((8, 64, width), grads.dtype), eight] if fetch else []
    if received:
        lead = (4, 2) if place is x_yh else (8,)
        out = pltpu.HBM(lead + (64, columns), jnp.float32)
        scratch += [pltpu.VMEM((8, 64, columns), jnp.float32), eight]
    else:
        out = jax.ShapeDtypeStruct((512, columns), jnp.float32)
    part = pl.BlockSpec((8, 1, 64, width), lambda i, pick: (0, pick[0], 0, 0))
    return call(
        functools.partial(product_kernel, fetch, place),
        [out],
        [HBM if received else None],
        [HBM if fetch else part, None] + [None] * len(received),
        half.reshape(1),
        in_hbm(grads) if fetch else grads,
        weight,
        *received,
        flops=tokens * columns * width,
        scratch=scratch,
    )[0]


def sum_along_x_kernel(pick, parts, near, far, held, semaphores):
    copy_all(
        [(parts.at[i % 4, i // 4], held.at[i // 4, i % 4]) for i in range(8)],
        semaphores,
    )
    first, second = jnp.sum(held[0], axis=0), jnp.sum(held[1], axis=0)
    near[...] = jnp.where(pick[0] == 0, first, second)
    far[...] = jnp.where(pick[0] == 0, second, first)


def sum_along_x(yh, parts):
    columns = parts.shape[-1]
    return call(
        sum_along_x_kernel,
        [jax.ShapeDtypeStruct((64, columns), jnp.float32)] * 2,
        [None] * 2,
        [HBM],
        yh.reshape(1),
        in_hbm(parts),
        scratch=[
            pltpu.VMEM((2, 4, 64, columns), jnp.float32),
            pltpu.SemaphoreType.DMA((8,)),
        ],
    )


def finish_kernel(pick, *refs):
    parts, outs = refs[:4], refs[4:]
    for near, far, out in zip(parts[::2], parts[1::2], outs):
        out[...] = (near[...] + far[...])[:, : out.shape[1]].astype(jnp.bfloat16)


def momentum_kernel(
    first, pick, inputs, inputs_theirs, grads, grads_theirs, moment, step, momentum
):
    rows = pl.ds(first, moment.shape[0])
    tokens = grads.shape[0] * grads.shape[2]
    width = grads.shape[-1]
    gradient = rows_product(
        inputs[..., rows].reshape(tokens, -1), grads[...].reshape(tokens, width)
    ) + rows_product(
        inputs_theirs[..., rows].reshape(tokens, -1),
        grads_theirs[...].reshape(tokens, width),
    )
    gradient = gradient * (1.0 / math.sqrt(float(2 * tokens)))
    held = moment[...].astype(jnp.float32)
    blended = 0.9 * held + 0.1 * gradient
    step[...] = (blended / jnp.sqrt(blended * blended + 0.01)).astype(jnp.bfloat16)
    momentum[...] = (0.99 * held + 0.01 * gradient).astype(jnp.bfloat16)


def momentum_step(core, inputs, inputs_theirs, first, grads, moment):
    tokens, width = grads.shape
    grads = grads.reshape(tokens // 128, 2, 64, width)
    block = (tokens // 128, 1, 64, width)
    return call(
        functools.partial(momentum_kernel, first),
        [jax.ShapeDtypeStruct(moment.shape, jnp.bfloat16)] * 2,
        [None] * 2,
        [
            None,
            None,
            pl.BlockSpec(block, lambda i, pick: (0, pick[0], 0, 0)),
            pl.BlockSpec(block, lambda i, pick: (0, 1 - pick[0], 0, 0)),
            None,
        ],
        core.reshape(1),
        inputs,
        inputs_theirs,
        grads,
        grads,
        moment,
        flops=2 * tokens * moment.size,
    )


def on_device(
    block_input,
    context,
    query_grad,
    output_grad,
    query_weight,
    query_moment,
    output_weight,
    output_moment,
):
    core, yh = lax.axis_index("core"), lax.axis_index("yh")
    width = query_grad.shape[1]
    grads = side_by_side(query_grad, output_grad)
    grads = lax.all_gather(grads, "yl", axis=0, tiled=True)
    output_part, block_input, context = lax.optimization_barrier(
        (grads[:, PAD:], block_input, context)
    )
    output_all = lax.all_gather(output_part, "z", axis=0, tiled=True)
    inputs = side_by_side(block_input, context)
    inputs = jnp.broadcast_to(inputs[None], (8,) + inputs.shape)
    inputs = lax.all_to_all(inputs, ("yh", "x"), 0, 0, tiled=True)
    query_all = lax.all_gather(grads[:, :width], "z", axis=0, tiled=True)
    query_all, inputs = lax.optimization_barrier((query_all, inputs))
    query_theirs = token_half(1 - core, query_all, query_weight)
    query_theirs = lax.ppermute(query_theirs, "core", SWAP)
    inputs_theirs = lax.ppermute(inputs, "core", SWAP)
    query_pair = token_half(core, query_all, query_weight, query_theirs, place=x_yh)
    query_pair, inputs_theirs = lax.optimization_barrier((query_pair, inputs_theirs))
    query_parts = lax.all_to_all(query_pair, "x", 0, 0, tiled=True)
    output_theirs = token_half(1 - core, output_all, output_weight, fetch=True)
    output_theirs = lax.ppermute(output_theirs, "core", SWAP)
    output_pair = token_half(
        core, output_all, output_weight, output_theirs, fetch=True, place=x_yh
    )
    query_step, query_momentum = momentum_step(
        core, inputs, inputs_theirs, 0, query_all, query_moment
    )
    output_step, output_momentum = momentum_step(
        core, inputs, inputs_theirs, PAD, output_all, output_moment
    )
    query_parts, output_pair, query_step, output_step = lax.optimization_barrier(
        (query_parts, output_pair, query_step, output_step)
    )
    output_parts = lax.all_to_all(output_pair, "x", 0, 0, tiled=True)
    query_near, query_far = sum_along_x(yh, query_parts)
    query_far = lax.ppermute(query_far, "yh", SWAP)
    output_near, output_far = sum_along_x(yh, output_parts)
    output_far = lax.ppermute(output_far, "yh", SWAP)
    input_grad, context_grad = call(
        finish_kernel,
        [
            jax.ShapeDtypeStruct(block_input.shape, jnp.bfloat16),
            jax.ShapeDtypeStruct(context.shape, jnp.bfloat16),
        ],
        [None] * 2,
        [None] * 4,
        jnp.zeros((1,), jnp.int32),
        query_near,
        query_far,
        output_near,
        output_far,
    )
    return (
        input_grad,
        context_grad,
        query_step,
        query_momentum,
        output_step,
        output_momentum,
    )


def solution(mesh):
    split = Mesh(mesh.devices.reshape(2, 4, 2, 8, 4), GX + GYZ)
    rows, columns = P(GX, GYZ), P(GYZ, GX)
    return jax.shard_map(
        on_device,
        mesh=split,
        in_specs=(rows, rows) + (columns,) * 6,
        out_specs=(rows, rows) + (columns,) * 4,
        check_vma=False,
    )
```

```python
import functools
import math

import jax
import jax.numpy as jnp
from jax import lax
from jax.experimental import pallas as pl
from jax.experimental.pallas import tpu as pltpu
from jax.sharding import Mesh, PartitionSpec as P

GX, GYZ = ("yh", "x", "core"), ("z", "yl")
SWAP = [(0, 1), (1, 0)]
PAD = 512
MIB = 2**20


def times_transposed(left, right):
    return lax.dot_general(
        left, right, (((1,), (1,)), ((), ())), preferred_element_type=jnp.float32
    )


def rows_product(left, right):
    return lax.dot_general(
        left, right, (((0,), (0,)), ((), ())), preferred_element_type=jnp.float32
    )


def lanes(columns):
    return -(-columns // 128) * 128


def side_by_side(left, right):
    gap = jnp.zeros((left.shape[0], PAD - left.shape[1]), left.dtype)
    return jnp.concatenate([left, gap, right], axis=1)


def call(
    kernel, out_shapes, out_specs, in_specs, pick, *operands, flops=0, scratch=()
):
    whole = lambda array: pl.BlockSpec(array.shape, lambda i, pick: (0,) * array.ndim)
    moved = sum(o.size * o.dtype.itemsize for o in operands)
    return pl.pallas_call(
        kernel,
        grid_spec=pltpu.PrefetchScalarGridSpec(
            num_scalar_prefetch=1,
            grid=(1,),
            scratch_shapes=scratch,
            in_specs=[spec or whole(o) for spec, o in zip(in_specs, operands)],
            out_specs=[spec or whole(o) for spec, o in zip(out_specs, out_shapes)],
        ),
        out_shape=out_shapes,
        compiler_params=pltpu.CompilerParams(vmem_limit_bytes=20 * MIB),
        cost_estimate=pl.CostEstimate(
            flops=flops, bytes_accessed=moved, transcendentals=0
        ),
    )(pick, *operands)


HBM = pl.BlockSpec(memory_space=pltpu.HBM)


def in_hbm(array):
    return pltpu.with_memory_space_constraint(array, pltpu.HBM)


def copy_all(pairs, semaphores):
    copies = [
        pltpu.make_async_copy(source, target, semaphores.at[i])
        for i, (source, target) in enumerate(pairs)
    ]
    for copy in copies:
        copy.start()
    for copy in copies:
        copy.wait()


def product_kernel(fetch, place, pick, grads, weight, *rest):
    rest, scratch = rest[: 1 + (place is not None)], rest[1 + (place is not None) :]
    scratch = list(scratch)
    if fetch:
        held, semaphores = scratch.pop(0), scratch.pop(0)
        copy_all([(grads.at[i, pick[0]], held.at[i]) for i in range(8)], semaphores)
    else:
        held = grads
    product = times_transposed(held[...].reshape(512, held.shape[-1]), weight[...])
    features = product.shape[1]
    out = rest[-1]
    gap = jnp.zeros((512, out.shape[-1] - features), jnp.float32)
    if place is None:
        out[:, :features] = product
        out[:, features:] = gap
        return
    sums, semaphores = scratch
    sums[:, :, :features] = (product + rest[0][:, :features]).reshape(8, 64, features)
    sums[:, :, features:] = gap.reshape(8, 64, -1)
    copy_all([(sums.at[i], out.at[place(i)]) for i in range(8)], semaphores)


def x_yh(chip):
    return (chip % 4, chip // 4)


def in_turn(chip):
    return (chip,)


def token_half(half, grads, weight, *received, fetch=False, place=None):
    tokens, width = grads.shape
    columns = lanes(weight.shape[0])
    grads = grads.reshape(8, 2, 64, width)
    eight = pltpu.SemaphoreType.DMA((8,))
    scratch = [pltpu.VMEM((8, 64, width), grads.dtype), eight] if fetch else []
    if received:
        lead = (4, 2) if place is x_yh else (8,)
        out = pltpu.HBM(lead + (64, columns), jnp.float32)
        scratch += [pltpu.VMEM((8, 64, columns), jnp.float32), eight]
    else:
        out = jax.ShapeDtypeStruct((512, columns), jnp.float32)
    part = pl.BlockSpec((8, 1, 64, width), lambda i, pick: (0, pick[0], 0, 0))
    return call(
        functools.partial(product_kernel, fetch, place),
        [out],
        [HBM if received else None],
        [HBM if fetch else part, None] + [None] * len(received),
        half.reshape(1),
        in_hbm(grads) if fetch else grads,
        weight,
        *received,
        flops=tokens * columns * width,
        scratch=scratch,
    )[0]


def sum_along_x_kernel(pick, parts, near, far, held, semaphores):
    copy_all(
        [(parts.at[i % 4, i // 4], held.at[i // 4, i % 4]) for i in range(8)],
        semaphores,
    )
    first, second = jnp.sum(held[0], axis=0), jnp.sum(held[1], axis=0)
    near[...] = jnp.where(pick[0] == 0, first, second)
    far[...] = jnp.where(pick[0] == 0, second, first)


def sum_along_x(yh, parts):
    columns = parts.shape[-1]
    return call(
        sum_along_x_kernel,
        [jax.ShapeDtypeStruct((64, columns), jnp.float32)] * 2,
        [None] * 2,
        [HBM],
        yh.reshape(1),
        in_hbm(parts),
        scratch=[
            pltpu.VMEM((2, 4, 64, columns), jnp.float32),
            pltpu.SemaphoreType.DMA((8,)),
        ],
    )


def finish_kernel(pick, *refs):
    parts, outs = refs[:4], refs[4:]
    for near, far, out in zip(parts[::2], parts[1::2], outs):
        out[...] = (near[...] + far[...])[:, : out.shape[1]].astype(jnp.bfloat16)


def momentum_kernel(
    first, pick, inputs, inputs_theirs, grads, grads_theirs, moment, step, momentum
):
    rows = pl.ds(first, moment.shape[0])
    tokens = grads.shape[0] * grads.shape[2]
    width = grads.shape[-1]
    gradient = rows_product(
        inputs[..., rows].reshape(tokens, -1), grads[...].reshape(tokens, width)
    ) + rows_product(
        inputs_theirs[..., rows].reshape(tokens, -1),
        grads_theirs[...].reshape(tokens, width),
    )
    gradient = gradient * (1.0 / math.sqrt(float(2 * tokens)))
    held = moment[...].astype(jnp.float32)
    blended = 0.9 * held + 0.1 * gradient
    step[...] = (blended / jnp.sqrt(blended * blended + 0.01)).astype(jnp.bfloat16)
    momentum[...] = (0.99 * held + 0.01 * gradient).astype(jnp.bfloat16)


def momentum_step(core, inputs, inputs_theirs, first, grads, moment):
    tokens, width = grads.shape
    grads = grads.reshape(tokens // 128, 2, 64, width)
    block = (tokens // 128, 1, 64, width)
    return call(
        functools.partial(momentum_kernel, first),
        [jax.ShapeDtypeStruct(moment.shape, jnp.bfloat16)] * 2,
        [None] * 2,
        [
            None,
            None,
            pl.BlockSpec(block, lambda i, pick: (0, pick[0], 0, 0)),
            pl.BlockSpec(block, lambda i, pick: (0, 1 - pick[0], 0, 0)),
            None,
        ],
        core.reshape(1),
        inputs,
        inputs_theirs,
        grads,
        grads,
        moment,
        flops=2 * tokens * moment.size,
    )


def on_device(
    block_input,
    context,
    query_grad,
    output_grad,
    query_weight,
    query_moment,
    output_weight,
    output_moment,
):
    core, yh = lax.axis_index("core"), lax.axis_index("yh")
    width = query_grad.shape[1]
    grads = side_by_side(query_grad, output_grad)
    grads = lax.all_gather(grads, "yl", axis=0, tiled=True)
    output_part, block_input, context = lax.optimization_barrier(
        (grads[:, PAD:], block_input, context)
    )
    output_all = lax.all_gather(output_part, "z", axis=0, tiled=True)
    inputs = side_by_side(block_input, context)
    inputs = jnp.broadcast_to(inputs[None], (8,) + inputs.shape)
    inputs = lax.all_to_all(inputs, ("yh", "x"), 0, 0, tiled=True)
    query_all = lax.all_gather(grads[:, :width], "z", axis=0, tiled=True)
    query_all, inputs = lax.optimization_barrier((query_all, inputs))
    query_theirs = token_half(1 - core, query_all, query_weight)
    query_theirs = lax.ppermute(query_theirs, "core", SWAP)
    query_pair = token_half(core, query_all, query_weight, query_theirs, place=x_yh)
    query_pair, inputs = lax.optimization_barrier((query_pair, inputs))
    query_parts = lax.all_to_all(query_pair, "x", 0, 0, tiled=True)
    output_theirs = token_half(1 - core, output_all, output_weight, fetch=True)
    output_theirs = lax.ppermute(output_theirs, "core", SWAP)
    inputs_theirs = lax.ppermute(inputs, "core", SWAP)
    output_pair = token_half(
        core, output_all, output_weight, output_theirs, fetch=True, place=x_yh
    )
    query_step, query_momentum = momentum_step(
        core, inputs, inputs_theirs, 0, query_all, query_moment
    )
    query_parts, output_pair, query_step = lax.optimization_barrier(
        (query_parts, output_pair, query_step)
    )
    output_parts = lax.all_to_all(output_pair, "x", 0, 0, tiled=True)
    query_near, query_far = sum_along_x(yh, query_parts)
    query_far = lax.ppermute(query_far, "yh", SWAP)
    output_near, output_far = sum_along_x(yh, output_parts)
    output_far = lax.ppermute(output_far, "yh", SWAP)
    output_step, output_momentum = momentum_step(
        core, inputs, inputs_theirs, PAD, output_all, output_moment
    )
    output_far, output_step = lax.optimization_barrier((output_far, output_step))
    input_grad, context_grad = call(
        finish_kernel,
        [
            jax.ShapeDtypeStruct(block_input.shape, jnp.bfloat16),
            jax.ShapeDtypeStruct(context.shape, jnp.bfloat16),
        ],
        [None] * 2,
        [None] * 4,
        jnp.zeros((1,), jnp.int32),
        query_near,
        query_far,
        output_near,
        output_far,
    )
    return (
        input_grad,
        context_grad,
        query_step,
        query_momentum,
        output_step,
        output_momentum,
    )


def solution(mesh):
    split = Mesh(mesh.devices.reshape(2, 4, 2, 8, 4), GX + GYZ)
    rows, columns = P(GX, GYZ), P(GYZ, GX)
    return jax.shard_map(
        on_device,
        mesh=split,
        in_specs=(rows, rows) + (columns,) * 6,
        out_specs=(rows, rows) + (columns,) * 4,
        check_vma=False,
    )
```

```python
import functools
import math

import jax
import jax.numpy as jnp
from jax import lax
from jax.experimental import pallas as pl
from jax.experimental.pallas import tpu as pltpu
from jax.sharding import Mesh, PartitionSpec as P

GX, GYZ = ("yh", "x", "core"), ("z", "yl")
SWAP = [(0, 1), (1, 0)]
PAD = 512
MIB = 2**20


def times_transposed(left, right):
    return lax.dot_general(
        left, right, (((1,), (1,)), ((), ())), preferred_element_type=jnp.float32
    )


def rows_product(left, right):
    return lax.dot_general(
        left, right, (((0,), (0,)), ((), ())), preferred_element_type=jnp.float32
    )


def lanes(columns):
    return -(-columns // 128) * 128


def side_by_side(left, right):
    gap = jnp.zeros((left.shape[0], PAD - left.shape[1]), left.dtype)
    return jnp.concatenate([left, gap, right], axis=1)


def call(
    kernel, out_shapes, out_specs, in_specs, pick, *operands, flops=0, scratch=()
):
    whole = lambda array: pl.BlockSpec(array.shape, lambda i, pick: (0,) * array.ndim)
    moved = sum(o.size * o.dtype.itemsize for o in operands)
    return pl.pallas_call(
        kernel,
        grid_spec=pltpu.PrefetchScalarGridSpec(
            num_scalar_prefetch=1,
            grid=(1,),
            scratch_shapes=scratch,
            in_specs=[spec or whole(o) for spec, o in zip(in_specs, operands)],
            out_specs=[spec or whole(o) for spec, o in zip(out_specs, out_shapes)],
        ),
        out_shape=out_shapes,
        compiler_params=pltpu.CompilerParams(vmem_limit_bytes=20 * MIB),
        cost_estimate=pl.CostEstimate(
            flops=flops, bytes_accessed=moved, transcendentals=0
        ),
    )(pick, *operands)


HBM = pl.BlockSpec(memory_space=pltpu.HBM)


def in_hbm(array):
    return pltpu.with_memory_space_constraint(array, pltpu.HBM)


def copy_all(pairs, semaphores):
    copies = [
        pltpu.make_async_copy(source, target, semaphores.at[i])
        for i, (source, target) in enumerate(pairs)
    ]
    for copy in copies:
        copy.start()
    for copy in copies:
        copy.wait()


def product_kernel(fetch, place, pick, grads, weight, *rest):
    rest, scratch = rest[: 1 + (place is not None)], rest[1 + (place is not None) :]
    scratch = list(scratch)
    if fetch:
        held, semaphores = scratch.pop(0), scratch.pop(0)
        copy_all([(grads.at[i, pick[0]], held.at[i]) for i in range(8)], semaphores)
    else:
        held = grads
    product = times_transposed(held[...].reshape(512, held.shape[-1]), weight[...])
    features = product.shape[1]
    out = rest[-1]
    gap = jnp.zeros((512, out.shape[-1] - features), jnp.float32)
    if place is None:
        out[:, :features] = product
        out[:, features:] = gap
        return
    sums, semaphores = scratch
    sums[:, :, :features] = (product + rest[0][:, :features]).reshape(8, 64, features)
    sums[:, :, features:] = gap.reshape(8, 64, -1)
    copy_all([(sums.at[i], out.at[place(i)]) for i in range(8)], semaphores)


def x_yh(chip):
    return (chip % 4, chip // 4)


def in_turn(chip):
    return (chip,)


def token_half(half, grads, weight, *received, fetch=False, place=None):
    tokens, width = grads.shape
    columns = lanes(weight.shape[0])
    grads = grads.reshape(8, 2, 64, width)
    eight = pltpu.SemaphoreType.DMA((8,))
    scratch = [pltpu.VMEM((8, 64, width), grads.dtype), eight] if fetch else []
    if received:
        lead = (4, 2) if place is x_yh else (8,)
        out = pltpu.HBM(lead + (64, columns), jnp.float32)
        scratch += [pltpu.VMEM((8, 64, columns), jnp.float32), eight]
    else:
        out = jax.ShapeDtypeStruct((512, columns), jnp.float32)
    part = pl.BlockSpec((8, 1, 64, width), lambda i, pick: (0, pick[0], 0, 0))
    return call(
        functools.partial(product_kernel, fetch, place),
        [out],
        [HBM if received else None],
        [HBM if fetch else part, None] + [None] * len(received),
        half.reshape(1),
        in_hbm(grads) if fetch else grads,
        weight,
        *received,
        flops=tokens * columns * width,
        scratch=scratch,
    )[0]


def sum_along_x_kernel(pick, parts, near, far, held, semaphores):
    copy_all(
        [(parts.at[i % 4, i // 4], held.at[i // 4, i % 4]) for i in range(8)],
        semaphores,
    )
    first, second = jnp.sum(held[0], axis=0), jnp.sum(held[1], axis=0)
    near[...] = jnp.where(pick[0] == 0, first, second)
    far[...] = jnp.where(pick[0] == 0, second, first)


def sum_along_x(yh, parts):
    columns = parts.shape[-1]
    return call(
        sum_along_x_kernel,
        [jax.ShapeDtypeStruct((64, columns), jnp.float32)] * 2,
        [None] * 2,
        [HBM],
        yh.reshape(1),
        in_hbm(parts),
        scratch=[
            pltpu.VMEM((2, 4, 64, columns), jnp.float32),
            pltpu.SemaphoreType.DMA((8,)),
        ],
    )


def finish_kernel(pick, *refs):
    parts, outs = refs[:4], refs[4:]
    for near, far, out in zip(parts[::2], parts[1::2], outs):
        out[...] = (near[...] + far[...])[:, : out.shape[1]].astype(jnp.bfloat16)


def momentum_kernel(
    first, pick, inputs, inputs_theirs, grads, grads_theirs, moment, step, momentum
):
    rows = pl.ds(first, moment.shape[0])
    tokens = grads.shape[0] * grads.shape[2]
    width = grads.shape[-1]
    gradient = rows_product(
        inputs[..., rows].reshape(tokens, -1), grads[...].reshape(tokens, width)
    ) + rows_product(
        inputs_theirs[..., rows].reshape(tokens, -1),
        grads_theirs[...].reshape(tokens, width),
    )
    gradient = gradient * (1.0 / math.sqrt(float(2 * tokens)))
    held = moment[...].astype(jnp.float32)
    blended = 0.9 * held + 0.1 * gradient
    step[...] = (blended / jnp.sqrt(blended * blended + 0.01)).astype(jnp.bfloat16)
    momentum[...] = (0.99 * held + 0.01 * gradient).astype(jnp.bfloat16)


def momentum_step(core, inputs, inputs_theirs, first, grads, moment):
    tokens, width = grads.shape
    grads = grads.reshape(tokens // 128, 2, 64, width)
    block = (tokens // 128, 1, 64, width)
    return call(
        functools.partial(momentum_kernel, first),
        [jax.ShapeDtypeStruct(moment.shape, jnp.bfloat16)] * 2,
        [None] * 2,
        [
            None,
            None,
            pl.BlockSpec(block, lambda i, pick: (0, pick[0], 0, 0)),
            pl.BlockSpec(block, lambda i, pick: (0, 1 - pick[0], 0, 0)),
            None,
        ],
        core.reshape(1),
        inputs,
        inputs_theirs,
        grads,
        grads,
        moment,
        flops=2 * tokens * moment.size,
    )


def on_device(
    block_input,
    context,
    query_grad,
    output_grad,
    query_weight,
    query_moment,
    output_weight,
    output_moment,
):
    core, yh = lax.axis_index("core"), lax.axis_index("yh")
    width = query_grad.shape[1]
    grads = side_by_side(query_grad, output_grad)
    grads = lax.all_gather(grads, "yl", axis=0, tiled=True)
    output_part, block_input, context = lax.optimization_barrier(
        (grads[:, PAD:], block_input, context)
    )
    output_all = lax.all_gather(output_part, "z", axis=0, tiled=True)
    inputs = side_by_side(block_input, context)
    inputs = jnp.broadcast_to(inputs[None], (8,) + inputs.shape)
    inputs = lax.all_to_all(inputs, ("yh", "x"), 0, 0, tiled=True)
    query_all = lax.all_gather(grads[:, :width], "z", axis=0, tiled=True)
    query_all, inputs = lax.optimization_barrier((query_all, inputs))
    query_theirs = token_half(1 - core, query_all, query_weight)
    query_theirs = lax.ppermute(query_theirs, "core", SWAP)
    query_pair = token_half(core, query_all, query_weight, query_theirs, place=x_yh)
    query_parts = lax.all_to_all(query_pair, "x", 0, 0, tiled=True)
    output_theirs = token_half(1 - core, output_all, output_weight, fetch=True)
    output_theirs = lax.ppermute(output_theirs, "core", SWAP)
    inputs_theirs = lax.ppermute(inputs, "core", SWAP)
    output_pair = token_half(
        core, output_all, output_weight, output_theirs, fetch=True, place=x_yh
    )
    query_step, query_momentum = momentum_step(
        core, inputs, inputs_theirs, 0, query_all, query_moment
    )
    output_step, output_momentum = momentum_step(
        core, inputs, inputs_theirs, PAD, output_all, output_moment
    )
    query_parts, output_pair, query_step, output_step = lax.optimization_barrier(
        (query_parts, output_pair, query_step, output_step)
    )
    output_parts = lax.all_to_all(output_pair, "x", 0, 0, tiled=True)
    query_near, query_far = sum_along_x(yh, query_parts)
    query_far = lax.ppermute(query_far, "yh", SWAP)
    output_near, output_far = sum_along_x(yh, output_parts)
    output_far = lax.ppermute(output_far, "yh", SWAP)
    input_grad, context_grad = call(
        finish_kernel,
        [
            jax.ShapeDtypeStruct(block_input.shape, jnp.bfloat16),
            jax.ShapeDtypeStruct(context.shape, jnp.bfloat16),
        ],
        [None] * 2,
        [None] * 4,
        jnp.zeros((1,), jnp.int32),
        query_near,
        query_far,
        output_near,
        output_far,
    )
    return (
        input_grad,
        context_grad,
        query_step,
        query_momentum,
        output_step,
        output_momentum,
    )


def solution(mesh):
    split = Mesh(mesh.devices.reshape(2, 4, 2, 8, 4), GX + GYZ)
    rows, columns = P(GX, GYZ), P(GYZ, GX)
    return jax.shard_map(
        on_device,
        mesh=split,
        in_specs=(rows, rows) + (columns,) * 6,
        out_specs=(rows, rows) + (columns,) * 4,
        check_vma=False,
    )
```
